256 devices in a mesh: dp: 4 (over x_lo, core), expert: 64 (over x_hi, y, z).
Axes of the slice: x: 4 (x_hi: 2, x_lo: 2; x = x_hi * 2 + x_lo), y: 4, z: 8, core: 2. Of those that a mesh axis runs over, the one named last changes fastest.
Arguments:
- out_grad: bfloat16 [32768, 2048], P(('dp', 'expert')), may hold values from -0.59765625 to 0.59765625
- expert_ids: int32 [32768, 2], P(('dp', 'expert')), may hold values from 0 to 63, all different within a row; in each aligned block of 128 rows (0 to 127, 128 to 255, ...) at most 9 rows name the same one
- keep: int32 [32768, 2], P(('dp', 'expert')), may hold values 0 or 1
- probs: bfloat16 [32768, 2], P(('dp', 'expert')), may hold values from 0.099609375 to 1
- gate_saved: bfloat16 [4, 64, 64, 9, 1408], P('dp', 'expert'), may hold values from -6 to 6
- up_saved: bfloat16 [4, 64, 64, 9, 1408], P('dp', 'expert'), may hold values from -6 to 6
- down_weight: bfloat16 [64, 1408, 2048], P('expert', 'dp'), may hold values from -0.15625 to 0.15625
Outputs:
- weight_grad: bfloat16 [64, 1408, 2048], P('expert', 'dp')
- gate_grad: bfloat16 [4, 64, 64, 9, 1408], P('dp', 'expert')
- up_grad: bfloat16 [4, 64, 64, 9, 1408], P('dp', 'expert')
- prob_grad: float32 [32768, 2], P(('dp', 'expert'))
The draws below stay inside these ranges and needn't reach their ends.
Inputs may be any that keep to these rules, and one draw needn't show every extreme that they name: `expert_ids`: among the 128 rows of one device, no expert is named by more than 9 rows, a bound that some block reaches; a row names 2 different experts.
All inputs are finite; a program needn't handle non-finite values. No bound on the sum of `keep` on one device may be relied on, other than what follows from the above.
Results may differ from the reference program's by a relative error of at most 0.015.
Values may be sent and summed in bfloat16 or wider, within the bound.
No kernel may reach another device: no remote copies, remote signals or barrier semaphores. Data moves between devices by JAX's collectives and lax.ppermute only.
A program may use at most 128 MiB of HBM per device.

```python
import math
import jax
import jax.numpy as jnp
import numpy as np
from jax import lax

D = 2048
FF = 1408
TOK_DEV = 128
TOP = 2
EXPERTS = 64
CAP = 9
TOKENS = 32768
N_DP = 4
N_EXPERT = 64


def touch_ends(array, rng, smallest, top_value):
    longest = array.shape.index(max(array.shape))
    spots = []
    for shift in (0, 1):
        where = [jax.random.randint(jax.random.fold_in(rng, axis), (), 0, length) for axis, length in enumerate(array.shape)]
        where[longest] = (where[longest] + shift) % array.shape[longest]
        spots.append(tuple(where))
    return array.at[spots[0]].set(smallest).at[spots[1]].set(top_value)


def shard_levels(key, shape, cuts, smallest, top_value):
    factor_of = 1.0
    for dim, shards_of in cuts:
        draws = jax.random.uniform(jax.random.fold_in(jax.random.fold_in(key, 6), dim), (shards_of,), jnp.float32, smallest / len(cuts), top_value / len(cuts))
        factor_of = factor_of * jnp.repeat(jnp.exp(draws), shape[dim] // shards_of).reshape((-1,) + (1,) * (len(shape) - 1 - dim))
    return factor_of


def shared_out(own_key, own, number, rows, amount, top, most, skew):
    order = jax.random.permutation(own_key, amount)
    crowded, usual = portions_of(amount, rows * top, most, skew, True), portions_of(amount, rows * top, most, skew, False)
    places = jnp.arange(amount)

    def named(tallies, turn):
        used = int((tallies > 0).sum())
        fixed = max(1, used // 4)
        passed = fixed + (places - fixed + turn * (used - fixed)) % max(1, amount - fixed)
        return jnp.zeros((amount,), jnp.int32).at[order[jnp.where(places < fixed, places, passed)]].set(jnp.asarray(tallies, jnp.int32))

    tallies = jnp.where(number % 4 == 0, named(crowded, number // 4), named(usual, number - number // 4 - 1))
    mixed = jax.random.permutation(jax.random.fold_in(own, 3), amount)
    donor, sink = mixed[0:amount // 2 * 2:2], mixed[1:amount // 2 * 2:2]
    room = jnp.minimum(tallies[donor] - 1, most - tallies[sink]) // 2
    room = jnp.where((donor == order[0]) | (sink == order[0]) | (tallies[sink] == 0), 0, jnp.maximum(room, 0))
    passed = jax.random.randint(jax.random.fold_in(own, 4), (amount // 2,), 0, 1 << 20) % (room + 1)
    tallies = tallies.at[donor].add(-passed).at[sink].add(passed)
    members = jnp.searchsorted(jnp.cumsum(tallies), jnp.arange(rows * top), side="right").astype(jnp.int32)
    listing = members.reshape(top, rows).T
    listing = listing[jax.random.permutation(jax.random.fold_in(own, 1), rows)]
    turn = jax.random.randint(jax.random.fold_in(own, 2), (rows, 1), 0, top)
    return jnp.take_along_axis(listing, (jnp.arange(top)[None, :] + turn) % top, axis=1)


def portions_of(count, total, most, skew, full):
    loads = [(1 << 20) // math.isqrt(standing ** skew) + 1 for standing in range(1, count + 1)]
    largest = most if full else min(most, max(-(-total // count), total * loads[0] // sum(loads)))
    least = 1 if total - largest >= count - 1 else 0
    counts, rest = [largest] + [least] * (count - 1), total - largest - least * (count - 1)
    while rest > 0:
        candidates = [i for i in range(1, count) if counts[i] < largest] or [i for i in range(1, count) if counts[i] < most]
        pool, left = sum([loads[i] for i in candidates]), rest
        for i in candidates:
            extra = min(most - counts[i], max(1, left * loads[i] // pool), rest)
            counts[i] = counts[i] + extra
            rest = rest - extra
    return np.array(counts)


def bell_draw(own_key, dims, scale, limit, split=(), held_as=jnp.bfloat16):
    result = scale * jax.random.normal(own_key, dims, jnp.float32)
    if split:
        result = result * shard_levels(own_key, dims, split, -0.22, 0.18)
    return jnp.clip(result, -limit, limit).astype(held_as)


def setup_inputs(seed: int = 0) -> dict:
    streams_of = jax.random.split(jax.random.key(seed), 8)
    out_grad = bell_draw(streams_of[0], (TOKENS, D), 0.1, 0.59765625, ((0, 256),))
    expert_ids_keys = jax.random.split(jax.random.fold_in(streams_of[1], 1), TOKENS // TOK_DEV)
    expert_ids_turns = jax.random.permutation(jax.random.fold_in(streams_of[1], 3), TOKENS // TOK_DEV)
    expert_ids = jax.vmap(lambda own, number: shared_out(jax.random.fold_in(streams_of[1], 2), own, number, TOK_DEV, EXPERTS, TOP, CAP, 2))(expert_ids_keys, expert_ids_turns).reshape((TOKENS, TOP))
    keep = touch_ends((jax.random.randint(streams_of[2], (TOKENS, TOP), 0, 8) < 7).astype(jnp.int32), jax.random.fold_in(streams_of[2], 1), 0, 1)
    probs = jnp.clip(0.099609375 + 0.9003906 * jax.random.uniform(streams_of[3], (TOKENS, TOP), jnp.float32) ** shard_levels(streams_of[3], (TOKENS, TOP), ((0, 256),), -0.2, 0.2), 0.099609375, 1.0).astype(jnp.bfloat16)
    gate_saved = bell_draw(streams_of[4], (N_DP, EXPERTS, N_EXPERT, CAP, FF), 1.0, 6.0, ((0, 4), (1, 64)))
    up_saved = bell_draw(streams_of[5], (N_DP, EXPERTS, N_EXPERT, CAP, FF), 1.0, 6.0, ((0, 4), (1, 64)))
    down_weight = bell_draw(streams_of[6], (EXPERTS, FF, D), FF ** -0.5, 0.15625, ((0, 64), (1, 4)))
    return dict(out_grad=out_grad, expert_ids=expert_ids, keep=keep, probs=probs, gate_saved=gate_saved, up_saved=up_saved, down_weight=down_weight)


def silu_parts(gate):
    sig = jax.nn.sigmoid(gate)
    return gate * sig, sig * (1.0 + gate * (1.0 - sig))


def slot_table(ids_dev, keep_dev):
    flat_ids = ids_dev.reshape(-1).astype(jnp.int32)
    onehot = (flat_ids[:, None] == jnp.arange(EXPERTS, dtype=jnp.int32)[None, :]).astype(jnp.int32)
    before = jnp.cumsum(onehot, axis=0) - onehot
    slot = jnp.sum(before * onehot, axis=1).astype(jnp.int32)
    dest = jnp.where(keep_dev.reshape(-1) == 1, flat_ids * CAP + slot, EXPERTS * CAP).astype(jnp.int32)
    table = jnp.full((EXPERTS * CAP + 1,), -1, jnp.int32)
    table = table.at[dest].set(jnp.arange(TOK_DEV * TOP, dtype=jnp.int32))
    return table[:-1], dest


def reference(out_grad, expert_ids, keep, probs, gate_saved, up_saved, down_weight):
    ids = expert_ids.reshape(N_DP * N_EXPERT, TOK_DEV, TOP)
    kept = keep.reshape(N_DP * N_EXPERT, TOK_DEV, TOP)
    tables, dests = jax.vmap(slot_table)(ids, kept)
    tables = tables.reshape(N_DP, N_EXPERT, EXPERTS, CAP)
    dests = dests.reshape(N_DP, N_EXPERT, TOK_DEV * TOP)
    grads = out_grad.reshape(N_DP, N_EXPERT * TOK_DEV, D)
    weights = probs.reshape(N_DP, N_EXPERT * TOK_DEV * TOP)
    source = jnp.arange(N_EXPERT, dtype=jnp.int32)[:, None]
    rows = N_EXPERT * CAP

    def one_expert(expert):
        weight = down_weight[expert]

        def one_group(total, group):
            entries = tables[group][:, expert]
            live = (entries >= 0).reshape(rows)
            pair = jnp.maximum(entries, 0).astype(jnp.int32)
            token = (source * TOK_DEV + pair // TOP).reshape(-1).astype(jnp.int32)
            flat_pair = (source * TOK_DEV * TOP + pair).reshape(-1).astype(jnp.int32)
            grad_in = jnp.where(live[:, None], grads[group][token], jnp.zeros((), jnp.bfloat16))
            prob_in = jnp.where(live, weights[group][flat_pair], jnp.zeros((), jnp.bfloat16))
            gate = gate_saved[group, expert].reshape(rows, FF).astype(jnp.float32)
            up = up_saved[group, expert].reshape(rows, FF).astype(jnp.float32)
            act, slope = silu_parts(gate)
            hidden = (act * up).astype(jnp.bfloat16)
            outs = jnp.dot(hidden, weight, preferred_element_type=jnp.float32).astype(jnp.bfloat16)
            scores = jnp.sum(grad_in.astype(jnp.float32) * outs.astype(jnp.float32), axis=1)
            scaled = (prob_in.astype(jnp.float32)[:, None] * grad_in.astype(jnp.float32)).astype(jnp.bfloat16)
            hidden_grad = jnp.dot(scaled, weight.T, preferred_element_type=jnp.float32)
            gate_grad = (hidden_grad * up * slope).astype(jnp.bfloat16)
            up_grad = (hidden_grad * act).astype(jnp.bfloat16)
            total = total + jnp.dot(hidden.T, scaled, preferred_element_type=jnp.float32)
            return total, (gate_grad.reshape(N_EXPERT, CAP, FF), up_grad.reshape(N_EXPERT, CAP, FF), scores.reshape(N_EXPERT, CAP))

        total, (gate_part, up_part, score_part) = lax.scan(one_group, jnp.zeros((FF, D), jnp.float32), jnp.arange(N_DP, dtype=jnp.int32))
        return total.astype(jnp.bfloat16), gate_part, up_part, score_part

    weight_grad, gate_all, up_all, score_all = lax.map(one_expert, jnp.arange(EXPERTS, dtype=jnp.int32))
    gate_grad = jnp.transpose(gate_all, (1, 0, 2, 3, 4))
    up_grad = jnp.transpose(up_all, (1, 0, 2, 3, 4))
    scores = jnp.transpose(score_all, (1, 2, 0, 3)).reshape(N_DP, N_EXPERT, EXPERTS * CAP)
    scores = jnp.concatenate([scores, jnp.zeros((N_DP, N_EXPERT, 1), jnp.float32)], axis=2)
    prob_grad = jnp.take_along_axis(scores, dests, axis=2).reshape(TOKENS, TOP)
    return weight_grad, gate_grad, up_grad, prob_grad
```

```python
import functools

import jax
import jax.numpy as jnp
from jax import lax
from jax.experimental import pallas as pl
from jax.experimental.pallas import tpu as pltpu
from jax.sharding import PartitionSpec as P

LANES = 128
BF16 = jnp.bfloat16
F32 = jnp.float32
MIB = 1 << 20


def pack_kernel(groups, cap, ids_ref, keep_ref, probs_ref, grad_ref, send_ref, dest_ref, wide):
    top, rows = ids_ref.shape
    blocks = grad_ref.shape[1] // LANES
    span = cap * blocks
    at_row = lax.broadcasted_iota(jnp.int32, (rows, rows), 0)
    at_col = lax.broadcasted_iota(jnp.int32, (rows, rows), 1)
    ids = [ids_ref[k : k + 1, :].astype(F32) for k in range(top)]
    columns = [
        jnp.sum(jnp.where(at_row == at_col, ids[k], 0.0), axis=1, keepdims=True) for k in range(top)
    ]
    dests = []
    for k in range(top):
        same = sum(jnp.where(columns[m] == ids[k], 1.0, 0.0) for m in range(top))
        slot = jnp.sum(jnp.where(at_row < at_col, same, 0.0), axis=0, keepdims=True).astype(jnp.int32)
        dest = slot * groups + ids_ref[k : k + 1, :]
        dest = jnp.where(keep_ref[k : k + 1, :] == 1, dest, -1)
        dest_ref[k : k + 1, :] = dest
        dests.append(dest)
    probs = [probs_ref[k : k + 1, :].astype(F32) for k in range(top)]
    for c in range(cap):
        row = lax.broadcasted_iota(jnp.int32, (groups, rows), 0) + c * groups
        pick = sum(jnp.where(row == dests[k], probs[k], 0.0) for k in range(top)).astype(BF16)
        out = jnp.dot(pick, grad_ref[...], preferred_element_type=F32)
        for j in range(blocks):
            wide[pl.ds(c * blocks + j, groups, stride=span), :] = out[:, j * LANES : (j + 1) * LANES]
    send_ref[...] = wide[...].astype(BF16)


def hidden_kernel(gate_ref, up_ref, me_ref, after_ref, far_other, far_mine, near_other, near_mine, whole):
    part = far_other.shape[0]
    step = 128
    for lo in range(0, gate_ref.shape[1], step):
        gate = gate_ref[:, lo : lo + step].astype(F32)
        hidden = gate * (1.0 / (1.0 + jnp.exp(-gate))) * up_ref[:, lo : lo + step].astype(F32)
        whole[lo : lo + step, :] = hidden.T.astype(BF16)
    me = me_ref[0]
    for flip, out in ((3, far_other), (2, far_mine), (1, near_other), (0, near_mine)):
        share = me ^ flip
        out[...] = whole[pl.ds(pl.multiple_of(share * part, 16), part), :]


def unpack_kernel(groups, cap, recv_ref, *refs):
    scaled_ref, wide = refs[-2:]
    blocks = scaled_ref.shape[1] // LANES
    span = cap * blocks
    wide[...] = recv_ref[...].astype(F32)
    for c in range(cap):
        for j in range(blocks):
            scaled_ref[c * groups : (c + 1) * groups, j * LANES : (j + 1) * LANES] = wide[
                pl.ds(c * blocks + j, groups, stride=span), :
            ].astype(BF16)


def finish_kernel(near_ref, *refs):
    out_ref = refs[-1]
    half = refs[0].shape[1]
    for k, far in enumerate(refs[:-1]):
        at = slice(k * half, (k + 1) * half)
        out_ref[:, at] = (near_ref[:, at] + far[...].astype(F32)).astype(BF16)


def grads_kernel(step, flips, scaled_ref, gate_ref, up_ref, *refs):
    shares, me_ref = refs[: len(flips)], refs[len(flips)]
    gate_grad_ref, up_grad_ref, score_ref, block_ref = refs[-4:]
    part = shares[0].shape[0]
    for flip, share in zip(flips, shares):
        block_ref[pl.ds(pl.multiple_of((me_ref[0] ^ flip) * part, 16), part), :] = share[...]
    width = block_ref.shape[0]
    total = jnp.zeros((scaled_ref.shape[0], 1), F32)
    for lo in range(0, width, step):
        hi = min(lo + step, width)
        hidden_grad = lax.dot_general(
            scaled_ref[...], block_ref[lo:hi, :], (((1,), (1,)), ((), ())), preferred_element_type=F32
        )
        gate = gate_ref[:, lo:hi].astype(F32)
        up = up_ref[:, lo:hi].astype(F32)
        sig = 1.0 / (1.0 + jnp.exp(-gate))
        act = gate * sig
        hidden = (act * up).astype(BF16).astype(F32)
        gate_grad_ref[:, lo:hi] = (hidden_grad * up * (sig * (1.0 + gate * (1.0 - sig)))).astype(BF16)
        up_grad_ref[:, lo:hi] = (hidden_grad * act).astype(BF16)
        total = total + jnp.sum(hidden * hidden_grad, axis=1, keepdims=True)
    score_ref[...] = total


def pick_kernel(back_ref, dest_ref, probs_ref, out_ref):
    total = back_ref.shape[0]
    top, rows = dest_ref.shape
    row = lax.broadcasted_iota(jnp.int32, (total, rows), 0)
    for k in range(top):
        dest = dest_ref[k : k + 1, :]
        value = jnp.sum(jnp.where(row == dest, back_ref[...], 0.0), axis=0, keepdims=True)
        out_ref[k : k + 1, :] = jnp.where(dest >= 0, value / probs_ref[k : k + 1, :].astype(F32), 0.0)


VMEM = pl.BlockSpec(memory_space=pltpu.VMEM)
SMEM = pl.BlockSpec(memory_space=pltpu.SMEM)
HELD = pl.BlockSpec(memory_space=pl.ANY)


def call(kernel, shapes, scratch, flops, moved, args, scalars=(), after=()):
    return pl.pallas_call(
        kernel,
        out_shape=[jax.ShapeDtypeStruct(s, t) for s, t in shapes],
        in_specs=[VMEM] * len(args) + [SMEM] * len(scalars) + [HELD] * len(after),
        out_specs=[VMEM] * len(shapes),
        scratch_shapes=scratch,
        compiler_params=pltpu.CompilerParams(vmem_limit_bytes=48 * MIB),
        cost_estimate=pl.CostEstimate(flops=flops, bytes_accessed=moved, transcendentals=0),
    )(*args, *scalars, *after)


def local(out_grad, expert_ids, keep, probs, gate_saved, up_saved, down_weight):
    groups = lax.axis_size("expert")
    replicas = lax.axis_size("dp")
    tok_rows, top = expert_ids.shape
    cap = gate_saved.shape[3]
    width = out_grad.shape[1]
    part = down_weight.shape[1]
    ff = gate_saved.shape[4]
    total = groups * cap
    blocks = width // LANES
    me = lax.axis_index("dp")
    here = me.astype(jnp.int32).reshape(1)
    over_core = [(r, r ^ 1) for r in range(replicas)]
    over_chip = [(r, r ^ 2) for r in range(replicas)]

    own = down_weight[0]
    beside = lax.ppermute(own, "dp", over_chip)

    ids, kept, prob = expert_ids.T, keep.T, probs.T
    send, dest = call(
        functools.partial(pack_kernel, groups, cap),
        [((total * blocks, LANES), BF16), ((top, tok_rows), jnp.int32)],
        [pltpu.VMEM((total * blocks, LANES), F32)],
        2 * total * tok_rows * width,
        6 * total * width,
        [ids, kept, prob, out_grad],
    )
    recv = lax.all_to_all(
        send.reshape(groups, cap * blocks, LANES), "expert", split_axis=0, concat_axis=0, tiled=True
    )

    gate = jnp.transpose(gate_saved[0, 0], (1, 0, 2)).reshape(total, ff)
    up = jnp.transpose(up_saved[0, 0], (1, 0, 2)).reshape(total, ff)
    pieces = call(
        hidden_kernel,
        [((part, total), BF16)] * 4,
        [pltpu.VMEM((ff, total), BF16)],
        20 * total * ff,
        20 * total * ff,
        [gate, up],
        [here],
        [dest],
    )
    far_other, far_mine, near_other, near_mine = pieces

    own, beside, _ = lax.optimization_barrier((own, beside, far_other))
    others = [lax.ppermute(own, "dp", over_core), lax.ppermute(beside, "dp", over_core)]

    (scaled,) = call(
        functools.partial(unpack_kernel, groups, cap),
        [((total, width), BF16)],
        [pltpu.VMEM((total * blocks, LANES), F32)],
        0,
        6 * total * width,
        [recv.reshape(total * blocks, LANES)],
        (),
        pieces,
    )

    def product(left, right):
        return jnp.dot(left, right, preferred_element_type=F32)

    halves = 2
    half = width // halves
    cols = [scaled[:, k * half : (k + 1) * half] for k in range(halves)]
    far = []
    for k in range(halves):
        got = lax.ppermute(product(far_other, cols[k]).astype(BF16), "dp", over_core)
        far.append((product(far_mine, cols[k]) + got.astype(F32)).astype(BF16))
    crossed = [lax.ppermute(f, "dp", over_chip) for f in far]
    got = lax.ppermute(product(near_other, scaled).astype(BF16), "dp", over_core)
    near = product(near_mine, scaled) + got.astype(F32)

    gate_grad, up_grad, score = call(
        functools.partial(grads_kernel, 256, (0, 2, 1, 3)),
        [((total, ff), BF16), ((total, ff), BF16), ((total, 1), F32)],
        [pltpu.VMEM((ff, width), BF16)],
        2 * total * width * ff,
        2 * (total * width + ff * width + 4 * total * ff),
        [scaled, gate, up, own, beside, *others],
        [here],
        far,
    )
    back = lax.all_to_all(
        score.reshape(cap, groups).T.reshape(groups, 1, cap), "expert", split_axis=0, concat_axis=0, tiled=True
    )
    (prob_grad,) = call(
        pick_kernel,
        [((top, tok_rows), F32)],
        [],
        total * tok_rows,
        total * LANES * 4,
        [back.reshape(groups, cap).T.reshape(total, 1), dest, prob],
    )
    (weight_grad,) = call(
        finish_kernel,
        [((part, width), BF16)],
        [],
        part * width,
        8 * part * width,
        [near, *crossed],
    )

    def bins(x):
        return jnp.transpose(x.reshape(cap, groups, ff), (1, 0, 2)).reshape(gate_saved.shape)

    return weight_grad[None], bins(gate_grad), bins(up_grad), prob_grad.T


def solution(mesh):
    placed = (
        P(("dp", "expert"), None),
        P(("dp", "expert"), None),
        P(("dp", "expert"), None),
        P(("dp", "expert"), None),
        P("dp", "expert", None, None, None),
        P("dp", "expert", None, None, None),
        P("expert", "dp", None),
    )
    return jax.shard_map(
        local,
        mesh=mesh,
        in_specs=placed,
        out_specs=(
            P("expert", "dp", None),
            P("dp", "expert", None, None, None),
            P("dp", "expert", None, None, None),
            P(("dp", "expert"), None),
        ),
        check_vma=False,
    )
```

```python
import functools

import jax
import jax.numpy as jnp
from jax import lax
from jax.experimental import pallas as pl
from jax.experimental.pallas import tpu as pltpu
from jax.sharding import PartitionSpec as P

LANES = 128
BF16 = jnp.bfloat16
F32 = jnp.float32
MIB = 1 << 20


def pack_kernel(groups, cap, ids_ref, keep_ref, probs_ref, grad_ref, send_ref, dest_ref, wide):
    top, rows = ids_ref.shape
    blocks = grad_ref.shape[1] // LANES
    span = cap * blocks
    turn = pl.program_id(0)

    @pl.when(turn == 0)
    def _():
        at_row = lax.broadcasted_iota(jnp.int32, (rows, rows), 0)
        at_col = lax.broadcasted_iota(jnp.int32, (rows, rows), 1)
        ids = [ids_ref[k : k + 1, :].astype(F32) for k in range(top)]
        columns = [
            jnp.sum(jnp.where(at_row == at_col, ids[k], 0.0), axis=1, keepdims=True) for k in range(top)
        ]
        for k in range(top):
            same = sum(jnp.where(columns[m] == ids[k], 1.0, 0.0) for m in range(top))
            slot = jnp.sum(jnp.where(at_row < at_col, same, 0.0), axis=0, keepdims=True).astype(jnp.int32)
            dest = slot * groups + ids_ref[k : k + 1, :]
            dest_ref[k : k + 1, :] = jnp.where(keep_ref[k : k + 1, :] == 1, dest, -1)

    some = send_ref.shape[0] // span
    expert = lax.broadcasted_iota(jnp.int32, (some, rows), 0) + turn * some
    probs = [probs_ref[k : k + 1, :].astype(F32) for k in range(top)]
    picks = [
        sum(jnp.where(expert + c * groups == dest_ref[k : k + 1, :], probs[k], 0.0) for k in range(top))
        for c in range(cap)
    ]
    out = jnp.dot(jnp.concatenate(picks, axis=0).astype(BF16), grad_ref[...], preferred_element_type=F32)
    for c in range(cap):
        for j in range(blocks):
            wide[pl.ds(c * blocks + j, some, stride=span), :] = out[
                c * some : (c + 1) * some, j * LANES : (j + 1) * LANES
            ]
    send_ref[...] = wide[...].astype(BF16)


def hidden_kernel(me_ref, gate_ref, up_ref, after_ref, *refs):
    pieces, token_ref, whole = refs[:-2], refs[-2], refs[-1]
    step = gate_ref.shape[1]
    turn = pl.program_id(0)
    gate = gate_ref[...].astype(F32)
    hidden = gate * (1.0 / (1.0 + jnp.exp(-gate))) * up_ref[...].astype(F32)
    whole[pl.ds(pl.multiple_of(turn * step, step), step), :] = hidden.T.astype(BF16)

    @pl.when(turn == pl.num_programs(0) - 1)
    def _():
        size = pieces[0].shape[0]
        cuts = len(pieces) // 4
        token_ref[...] = jnp.zeros_like(token_ref)
        for at, out in enumerate(pieces):
            flip, cut = 3 - at // cuts, at % cuts
            first = (me_ref[0] ^ flip) * (size * cuts) + cut * size
            out[...] = whole[pl.ds(pl.multiple_of(first, 16), size), :]


def unpack_kernel(groups, cap, recv_ref, *refs):
    cuts = (len(refs) - 7) // 2
    lefts, products = refs[:cuts], refs[cuts + 2 : 2 * cuts + 2]
    scaled_ref, wide, come, held, sems, left_sems = refs[cuts + 1], *refs[-5:]
    turns = come.shape[0]
    size = come.shape[1]
    loads = [
        pltpu.make_async_copy(recv_ref.at[pl.ds(i * size, size), :], come.at[i], sems.at[i])
        for i in range(turns)
    ]
    extra = [pltpu.make_async_copy(lefts[k], held.at[k], left_sems.at[k]) for k in range(cuts)]
    for load in loads + extra:
        load.start()
    blocks = scaled_ref.shape[1] // LANES
    span = cap * blocks
    for i in range(turns):
        loads[i].wait()
        wide[i * size : (i + 1) * size, :] = come[i].astype(F32)
    for c in range(cap):
        for j in range(blocks):
            scaled_ref[c * groups : (c + 1) * groups, j * LANES : (j + 1) * LANES] = wide[
                pl.ds(c * blocks + j, groups, stride=span), :
            ].astype(BF16)
    for k, out in enumerate(products):
        extra[k].wait()
        out[...] = jnp.dot(held[k], scaled_ref[...], preferred_element_type=F32).astype(BF16)


def grads_kernel(cap, step, flips, me_ref, scaled_ref, gate_ref, up_ref, *refs):
    gate_out, up_out, score_ref, token_ref, block_ref, gate_grad_ref, up_grad_ref, sems, out_sems = refs[-9:]
    stores = []
    shares = refs[: len(flips)]
    part = shares[0].shape[0]
    loads = []
    for at, flip in enumerate(flips):
        place = pl.ds(pl.multiple_of((me_ref[0] ^ flip) * part, 16), part)
        loads.append(pltpu.make_async_copy(shares[at], block_ref.at[place, :], sems.at[at]))
        loads[-1].start()
    for load in loads:
        load.wait()
    token_ref[...] = jnp.zeros_like(token_ref)
    width = block_ref.shape[0]
    total = 0.0
    for lo in range(0, width, step):
        hi = min(lo + step, width)
        hidden_grad = lax.dot_general(
            scaled_ref[...], block_ref[lo:hi, :], (((1,), (1,)), ((), ())), preferred_element_type=F32
        )
        for at in range(lo, hi, LANES):
            cols = slice(at, at + LANES)
            grad = hidden_grad[:, at - lo : at - lo + LANES]
            gate = gate_ref[:, cols].astype(F32)
            up = up_ref[:, cols].astype(F32)
            sig = 1.0 / (1.0 + jnp.exp(-gate))
            act = gate * sig
            up_grad = grad * act
            total = total + grad * (act * up).astype(BF16).astype(F32)
            gate_grad_ref[:, cols] = (grad * up * (sig * (1.0 + gate * (1.0 - sig)))).astype(BF16)
            up_grad_ref[:, cols] = up_grad.astype(BF16)
        here = (slice(None), pl.ds(lo, hi - lo))
        for side, (held, out) in enumerate(((gate_grad_ref, gate_out), (up_grad_ref, up_out))):
            stores.append(pltpu.make_async_copy(held.at[here], out.at[here], out_sems.at[side, lo // step]))
            stores[-1].start()
    scores = jnp.sum(total, axis=1, keepdims=True)
    groups = score_ref.shape[0]
    for c in range(cap):
        score_ref[:, c : c + 1] = scores[c * groups : (c + 1) * groups, :]
    for store in stores:
        store.wait()


def pick_kernel(back_ref, dest_ref, probs_ref, *refs):
    out_ref = refs[-1]
    groups, cap = back_ref.shape
    top, rows = dest_ref.shape
    row = lax.broadcasted_iota(jnp.int32, (groups, rows), 0)
    for k in range(top):
        dest = dest_ref[k : k + 1, :]
        value = jnp.zeros((groups, rows), F32)
        for c in range(cap):
            value = value + jnp.where(row + c * groups == dest, back_ref[:, c : c + 1], 0.0)
        value = jnp.sum(value, axis=0, keepdims=True)
        out_ref[k : k + 1, :] = jnp.where(dest >= 0, value / probs_ref[k : k + 1, :].astype(F32), 0.0)


def near_kernel(scaled_ref, *refs):
    cuts = (len(refs) - 2) // 2
    size = refs[0].shape[0]
    for k in range(cuts):
        total = jnp.dot(refs[k][...], scaled_ref[...], preferred_element_type=F32)
        refs[-1][k * size : (k + 1) * size, :] = total + refs[cuts + k][...].astype(F32)


def finish_kernel(near_ref, far_ref, *refs):
    refs[-1][...] = (near_ref[...] + far_ref[...].astype(F32)).astype(BF16)


SMEM = pl.BlockSpec(memory_space=pltpu.SMEM)
VMEM = pl.BlockSpec(memory_space=pltpu.VMEM)
HELD = pl.BlockSpec(memory_space=pl.ANY)
TOKEN = ((8, LANES), F32)


def fixed(shape):
    return pl.BlockSpec(shape, lambda i: (0,) * len(shape))


def rows_by(size, width):
    return pl.BlockSpec((size, width), lambda i: (i, 0))


def call(kernel, grid, args, outs, scratch, cost, after=(), aliases=None, limit=24):
    flops, moved = cost
    return pl.pallas_call(
        kernel,
        grid=() if grid is None else (grid,),
        out_shape=[jax.ShapeDtypeStruct(*o) for o, _ in outs],
        in_specs=[s for _, s in args] + [HELD] * len(after),
        out_specs=[s for _, s in outs],
        scratch_shapes=scratch,
        input_output_aliases=aliases or {},
        compiler_params=pltpu.CompilerParams(vmem_limit_bytes=limit * MIB),
        cost_estimate=pl.CostEstimate(flops=flops, bytes_accessed=moved, transcendentals=0),
    )(*[x for x, _ in args], *after)


def local(out_grad, expert_ids, keep, probs, gate_saved, up_saved, down_weight):
    groups = lax.axis_size("expert")
    replicas = lax.axis_size("dp")
    tok_rows, top = expert_ids.shape
    cap = gate_saved.shape[3]
    width = out_grad.shape[1]
    part = down_weight.shape[1]
    ff = gate_saved.shape[4]
    total = groups * cap
    blocks = width // LANES
    here = lax.axis_index("dp").astype(jnp.int32).reshape(1)
    over_core = [(r, r ^ 1) for r in range(replicas)]
    over_chip = [(r, r ^ 2) for r in range(replicas)]

    own = down_weight[0]
    beside = lax.ppermute(own, "dp", over_chip)
    own_there = lax.ppermute(own, "dp", over_core)

    ids, kept, prob = expert_ids.T, keep.T, probs.T
    small = fixed((top, tok_rows))
    turns = 4
    send, dest = call(
        functools.partial(pack_kernel, groups, cap),
        turns,
        [(ids, small), (kept, small), (prob, small), (out_grad, fixed((tok_rows, width)))],
        [
            (((total * blocks, LANES), BF16), rows_by(total * blocks // turns, LANES)),
            (((top, tok_rows), jnp.int32), small),
        ],
        [pltpu.VMEM((total * blocks // turns, LANES), F32)],
        (2 * total * tok_rows * width, 6 * total * width),
        limit=62,
    )
    recv = lax.all_to_all(
        send.reshape(groups, cap * blocks, LANES), "expert", split_axis=0, concat_axis=0, tiled=True
    )

    gate = jnp.transpose(gate_saved[0, 0], (1, 0, 2)).reshape(total, ff)
    up = jnp.transpose(up_saved[0, 0], (1, 0, 2)).reshape(total, ff)
    cuts = 2
    size = part // cuts
    by_lanes = pl.BlockSpec((total, LANES), lambda i: (0, i))
    *pieces, token = call(
        hidden_kernel,
        ff // LANES,
        [(here, SMEM), (gate, by_lanes), (up, by_lanes)],
        [(((size, total), BF16), fixed((size, total)))] * (4 * cuts)
        + [(TOKEN, fixed(TOKEN[0]))],
        [pltpu.VMEM((ff, total), BF16)],
        (20 * total * ff, 8 * total * ff),
        [dest],
    )
    far_other, far_mine, near_other, near_mine = [pieces[k * cuts : (k + 1) * cuts] for k in range(4)]

    left, half = fixed((size, total)), fixed((size, width))
    scaled, *first = call(
        functools.partial(unpack_kernel, groups, cap),
        None,
        [(recv.reshape(total * blocks, LANES), HELD)] + [(x, HELD) for x in far_other],
        [(((total, width), BF16), VMEM)] + [(((size, width), BF16), VMEM)] * cuts,
        [
            pltpu.VMEM((total * blocks, LANES), F32),
            pltpu.VMEM((turns, total * blocks // turns, LANES), BF16),
            pltpu.VMEM((cuts, size, total), BF16),
            pltpu.SemaphoreType.DMA((turns,)),
            pltpu.SemaphoreType.DMA((cuts,)),
        ],
        (2 * part * total * width, 8 * total * width),
        [token],
        limit=59,
    )

    def product(left):
        return jnp.dot(left, scaled, preferred_element_type=F32)

    def to_core(x):
        return lax.ppermute(x.astype(BF16), "dp", over_core)

    core_far = [to_core(x) for x in first]
    beside, first[0] = lax.optimization_barrier((beside, first[0]))
    others = [own_there, lax.ppermute(beside, "dp", over_core)]
    got = [to_core(product(x)) for x in near_other]
    far = [(product(x) + g.astype(F32)).astype(BF16) for x, g in zip(far_mine, core_far)]
    crossed = [lax.ppermute(x, "dp", over_chip) for x in far]

    gate_grad, up_grad, score, token = call(
        functools.partial(grads_kernel, cap, 2 * LANES, (0, 2, 1, 3)),
        None,
        [(here, SMEM)] + [(x, VMEM) for x in (scaled, gate, up)] + [(w, HELD) for w in (own, beside, *others)],
        [(((total, ff), BF16), HELD)] * 2 + [(((groups, cap), F32), VMEM), (TOKEN, VMEM)],
        [
            pltpu.VMEM((ff, width), BF16),
            pltpu.VMEM((total, ff), BF16),
            pltpu.VMEM((total, ff), BF16),
            pltpu.SemaphoreType.DMA((replicas,)),
            pltpu.SemaphoreType.DMA((2, -(-ff // (2 * LANES)))),
        ],
        (2 * total * width * ff, 2 * (total * width + ff * width + 4 * total * ff)),
        [far[-1]],
    )
    back = lax.all_to_all(
        score.reshape(groups, 1, cap), "expert", split_axis=0, concat_axis=0, tiled=True
    )
    (prob_grad,) = call(
        pick_kernel,
        1,
        [(back.reshape(groups, cap), fixed((groups, cap))), (dest, small), (prob, small)],
        [(((top, tok_rows), F32), small)],
        [],
        (total * tok_rows, total * LANES * 4),
        [token],
    )
    (near,) = call(
        near_kernel,
        1,
        [(scaled, fixed((total, width)))] + [(x, left) for x in near_mine] + [(x, half) for x in got],
        [(((part, width), F32), fixed((part, width)))],
        [],
        (2 * part * total * width, 8 * part * width),
        [token],
    )
    weight_grad = None
    for k in range(cuts):
        at = pl.BlockSpec((size, width), lambda i, k=k: (k, 0))
        (weight_grad,) = call(
            finish_kernel,
            1,
            [(near, at), (crossed[k], half)],
            [(((part, width), BF16), at)],
            [],
            (size * width, 8 * size * width),
            [] if k == 0 else [weight_grad],
            {} if k == 0 else {2: 0},
        )

    def bins(x):
        return jnp.transpose(x.reshape(cap, groups, ff), (1, 0, 2)).reshape(gate_saved.shape)

    return weight_grad[None], bins(gate_grad), bins(up_grad), prob_grad.T


def solution(mesh):
    placed = (
        P(("dp", "expert"), None),
        P(("dp", "expert"), None),
        P(("dp", "expert"), None),
        P(("dp", "expert"), None),
        P("dp", "expert", None, None, None),
        P("dp", "expert", None, None, None),
        P("expert", "dp", None),
    )
    return jax.shard_map(
        local,
        mesh=mesh,
        in_specs=placed,
        out_specs=(
            P("expert", "dp", None),
            P("dp", "expert", None, None, None),
            P("dp", "expert", None, None, None),
            P(("dp", "expert"), None),
        ),
        check_vma=False,
    )
```

```python
import functools

import jax
import jax.numpy as jnp
from jax import lax
from jax.experimental import pallas as pl
from jax.experimental.pallas import tpu as pltpu
from jax.sharding import PartitionSpec as P

LANES = 128
BF16 = jnp.bfloat16
F32 = jnp.float32
MIB = 1 << 20


def pack_kernel(groups, cap, ids_ref, keep_ref, probs_ref, grad_ref, send_ref, dest_ref, wide):
    top, rows = ids_ref.shape
    blocks = grad_ref.shape[1] // LANES
    span = cap * blocks
    turn = pl.program_id(0)

    @pl.when(turn == 0)
    def _():
        at_row = lax.broadcasted_iota(jnp.int32, (rows, rows), 0)
        at_col = lax.broadcasted_iota(jnp.int32, (rows, rows), 1)
        ids = [ids_ref[k : k + 1, :].astype(F32) for k in range(top)]
        columns = [
            jnp.sum(jnp.where(at_row == at_col, ids[k], 0.0), axis=1, keepdims=True) for k in range(top)
        ]
        for k in range(top):
            same = sum(jnp.where(columns[m] == ids[k], 1.0, 0.0) for m in range(top))
            slot = jnp.sum(jnp.where(at_row < at_col, same, 0.0), axis=0, keepdims=True).astype(jnp.int32)
            dest = slot * groups + ids_ref[k : k + 1, :]
            dest_ref[k : k + 1, :] = jnp.where(keep_ref[k : k + 1, :] == 1, dest, -1)

    some = send_ref.shape[0] // span
    expert = lax.broadcasted_iota(jnp.int32, (some, rows), 0) + turn * some
    probs = [probs_ref[k : k + 1, :].astype(F32) for k in range(top)]
    picks = [
        sum(jnp.where(expert + c * groups == dest_ref[k : k + 1, :], probs[k], 0.0) for k in range(top))
        for c in range(cap)
    ]
    out = jnp.dot(jnp.concatenate(picks, axis=0).astype(BF16), grad_ref[...], preferred_element_type=F32)
    for c in range(cap):
        for j in range(blocks):
            wide[pl.ds(c * blocks + j, some, stride=span), :] = out[
                c * some : (c + 1) * some, j * LANES : (j + 1) * LANES
            ]
    send_ref[...] = wide[...].astype(BF16)


def hidden_kernel(me_ref, gate_ref, up_ref, after_ref, *refs):
    pieces, token_ref, whole = refs[:-2], refs[-2], refs[-1]
    step = gate_ref.shape[1]
    turn = pl.program_id(0)
    gate = gate_ref[...].astype(F32)
    hidden = gate * (1.0 / (1.0 + jnp.exp(-gate))) * up_ref[...].astype(F32)
    whole[pl.ds(pl.multiple_of(turn * step, step), step), :] = hidden.T.astype(BF16)

    @pl.when(turn == pl.num_programs(0) - 1)
    def _():
        size = pieces[0].shape[0]
        cuts = len(pieces) // 4
        token_ref[...] = jnp.zeros_like(token_ref)
        for at, out in enumerate(pieces):
            flip, cut = 3 - at // cuts, at % cuts
            first = (me_ref[0] ^ flip) * (size * cuts) + cut * size
            out[...] = whole[pl.ds(pl.multiple_of(first, 16), size), :]


def unpack_kernel(groups, cap, recv_ref, *refs):
    cuts = (len(refs) - 7) // 2
    lefts, products = refs[:cuts], refs[cuts + 2 : 2 * cuts + 2]
    scaled_ref, wide, come, held, sems, left_sems = refs[cuts + 1], *refs[-5:]
    turns = come.shape[0]
    size = come.shape[1]
    loads = [
        pltpu.make_async_copy(recv_ref.at[pl.ds(i * size, size), :], come.at[i], sems.at[i])
        for i in range(turns)
    ]
    part = lefts[0].shape[0]
    extra = [
        pltpu.make_async_copy(lefts[k], held.at[pl.ds(k * part, part), :], left_sems.at[k]) for k in range(cuts)
    ]
    for load in loads + extra:
        load.start()
    blocks = scaled_ref.shape[1] // LANES
    span = cap * blocks
    for i in range(turns):
        loads[i].wait()
        wide[i * size : (i + 1) * size, :] = come[i].astype(F32)
    for c in range(cap):
        for j in range(blocks):
            scaled_ref[c * groups : (c + 1) * groups, j * LANES : (j + 1) * LANES] = wide[
                pl.ds(c * blocks + j, groups, stride=span), :
            ].astype(BF16)
    for load in extra:
        load.wait()
    whole = jnp.dot(held[...], scaled_ref[...], preferred_element_type=F32).astype(BF16)
    for k, out in enumerate(products):
        out[...] = whole[k * part : (k + 1) * part, :]


def grads_kernel(cap, step, flips, me_ref, scaled_ref, gate_ref, up_ref, *refs):
    gate_out, up_out, score_ref, token_ref, block_ref, gate_grad_ref, up_grad_ref = refs[-12:-5]
    act_ref, slope_ref, hidden_ref, sems, out_sems = refs[-5:]
    stores = []
    shares = refs[: len(flips)]
    part = shares[0].shape[0]
    loads = []
    for at, flip in enumerate(flips):
        place = pl.ds(pl.multiple_of((me_ref[0] ^ flip) * part, 16), part)
        loads.append(pltpu.make_async_copy(shares[at], block_ref.at[place, :], sems.at[at]))
        loads[-1].start()
    token_ref[...] = jnp.zeros_like(token_ref)
    width = block_ref.shape[0]
    for at in range(0, width, LANES):
        cols = slice(at, at + LANES)
        gate = gate_ref[:, cols].astype(F32)
        up = up_ref[:, cols].astype(F32)
        sig = 1.0 / (1.0 + jnp.exp(-gate))
        act = gate * sig
        act_ref[:, cols] = act
        slope_ref[:, cols] = up * (sig * (1.0 + gate * (1.0 - sig)))
        hidden_ref[:, cols] = (act * up).astype(BF16)
    for load in loads:
        load.wait()
    total = 0.0
    for lo in range(0, width, step):
        hi = min(lo + step, width)
        hidden_grad = lax.dot_general(
            scaled_ref[...], block_ref[lo:hi, :], (((1,), (1,)), ((), ())), preferred_element_type=F32
        )
        for at in range(lo, hi, LANES):
            cols = slice(at, at + LANES)
            grad = hidden_grad[:, at - lo : at - lo + LANES]
            total = total + grad * hidden_ref[:, cols].astype(F32)
            gate_grad_ref[:, cols] = (grad * slope_ref[:, cols]).astype(BF16)
            up_grad_ref[:, cols] = (grad * act_ref[:, cols]).astype(BF16)
        here = (slice(None), pl.ds(lo, hi - lo))
        for side, (held, out) in enumerate(((gate_grad_ref, gate_out), (up_grad_ref, up_out))):
            stores.append(pltpu.make_async_copy(held.at[here], out.at[here], out_sems.at[side, lo // step]))
            stores[-1].start()
    scores = jnp.sum(total, axis=1, keepdims=True)
    groups = score_ref.shape[0]
    for c in range(cap):
        score_ref[:, c : c + 1] = scores[c * groups : (c + 1) * groups, :]
    for store in stores:
        store.wait()


def pick_kernel(back_ref, dest_ref, probs_ref, *refs):
    out_ref = refs[-1]
    groups, cap = back_ref.shape
    top, rows = dest_ref.shape
    row = lax.broadcasted_iota(jnp.int32, (groups, rows), 0)
    for k in range(top):
        dest = dest_ref[k : k + 1, :]
        value = jnp.zeros((groups, rows), F32)
        for c in range(cap):
            value = value + jnp.where(row + c * groups == dest, back_ref[:, c : c + 1], 0.0)
        value = jnp.sum(value, axis=0, keepdims=True)
        out_ref[k : k + 1, :] = jnp.where(dest >= 0, value / probs_ref[k : k + 1, :].astype(F32), 0.0)


def near_kernel(scaled_ref, *refs):
    cuts = (len(refs) - 2) // 2
    size = refs[0].shape[0]
    for k in range(cuts):
        total = jnp.dot(refs[k][...], scaled_ref[...], preferred_element_type=F32)
        refs[-1][k * size : (k + 1) * size, :] = total + refs[cuts + k][...].astype(F32)


def finish_kernel(near_ref, far_ref, *refs):
    refs[-1][...] = (near_ref[...] + far_ref[...].astype(F32)).astype(BF16)


SMEM = pl.BlockSpec(memory_space=pltpu.SMEM)
VMEM = pl.BlockSpec(memory_space=pltpu.VMEM)
HELD = pl.BlockSpec(memory_space=pl.ANY)
TOKEN = ((8, LANES), F32)


def fixed(shape):
    return pl.BlockSpec(shape, lambda i: (0,) * len(shape))


def rows_by(size, width):
    return pl.BlockSpec((size, width), lambda i: (i, 0))


def call(kernel, grid, args, outs, scratch, cost, after=(), aliases=None, limit=24):
    flops, moved = cost
    return pl.pallas_call(
        kernel,
        grid=() if grid is None else (grid,),
        out_shape=[jax.ShapeDtypeStruct(*o) for o, _ in outs],
        in_specs=[s for _, s in args] + [HELD] * len(after),
        out_specs=[s for _, s in outs],
        scratch_shapes=scratch,
        input_output_aliases=aliases or {},
        compiler_params=pltpu.CompilerParams(vmem_limit_bytes=limit * MIB),
        cost_estimate=pl.CostEstimate(flops=flops, bytes_accessed=moved, transcendentals=0),
    )(*[x for x, _ in args], *after)


def local(out_grad, expert_ids, keep, probs, gate_saved, up_saved, down_weight):
    groups = lax.axis_size("expert")
    replicas = lax.axis_size("dp")
    tok_rows, top = expert_ids.shape
    cap = gate_saved.shape[3]
    width = out_grad.shape[1]
    part = down_weight.shape[1]
    ff = gate_saved.shape[4]
    total = groups * cap
    blocks = width // LANES
    here = lax.axis_index("dp").astype(jnp.int32).reshape(1)
    over_core = [(r, r ^ 1) for r in range(replicas)]
    over_chip = [(r, r ^ 2) for r in range(replicas)]

    own = down_weight[0]
    beside = lax.ppermute(own, "dp", over_chip)
    own_there = lax.ppermute(own, "dp", over_core)

    ids, kept, prob = expert_ids.T, keep.T, probs.T
    small = fixed((top, tok_rows))
    turns = 4
    send, dest = call(
        functools.partial(pack_kernel, groups, cap),
        turns,
        [(ids, small), (kept, small), (prob, small), (out_grad, fixed((tok_rows, width)))],
        [
            (((total * blocks, LANES), BF16), rows_by(total * blocks // turns, LANES)),
            (((top, tok_rows), jnp.int32), small),
        ],
        [pltpu.VMEM((total * blocks // turns, LANES), F32)],
        (2 * total * tok_rows * width, 6 * total * width),
        limit=62,
    )
    recv = lax.all_to_all(
        send.reshape(groups, cap * blocks, LANES), "expert", split_axis=0, concat_axis=0, tiled=True
    )

    gate = jnp.transpose(gate_saved[0, 0], (1, 0, 2)).reshape(total, ff)
    up = jnp.transpose(up_saved[0, 0], (1, 0, 2)).reshape(total, ff)
    cuts = 2
    size = part // cuts
    by_lanes = pl.BlockSpec((total, LANES), lambda i: (0, i))
    *pieces, token = call(
        hidden_kernel,
        ff // LANES,
        [(here, SMEM), (gate, by_lanes), (up, by_lanes)],
        [(((size, total), BF16), fixed((size, total)))] * (4 * cuts)
        + [(TOKEN, fixed(TOKEN[0]))],
        [pltpu.VMEM((ff, total), BF16)],
        (20 * total * ff, 8 * total * ff),
        [dest],
    )
    far_other, far_mine, near_other, near_mine = [pieces[k * cuts : (k + 1) * cuts] for k in range(4)]

    left, half = fixed((size, total)), fixed((size, width))
    scaled, *first = call(
        functools.partial(unpack_kernel, groups, cap),
        None,
        [(recv.reshape(total * blocks, LANES), HELD)] + [(x, HELD) for x in far_other],
        [(((total, width), BF16), VMEM)] + [(((size, width), BF16), VMEM)] * cuts,
        [
            pltpu.VMEM((total * blocks, LANES), F32),
            pltpu.VMEM((turns, total * blocks // turns, LANES), BF16),
            pltpu.VMEM((part, total), BF16),
            pltpu.SemaphoreType.DMA((turns,)),
            pltpu.SemaphoreType.DMA((cuts,)),
        ],
        (2 * part * total * width, 8 * total * width),
        [token],
        limit=59,
    )

    def product(left):
        return jnp.dot(left, scaled, preferred_element_type=F32)

    def to_core(x):
        return lax.ppermute(x.astype(BF16), "dp", over_core)

    core_far = [to_core(x) for x in first]
    beside, first[0] = lax.optimization_barrier((beside, first[0]))
    others = [own_there, lax.ppermute(beside, "dp", over_core)]
    got = [to_core(product(x)) for x in near_other]
    far = [(product(x) + g.astype(F32)).astype(BF16) for x, g in zip(far_mine, core_far)]
    crossed = [lax.ppermute(x, "dp", over_chip) for x in far]

    gate_grad, up_grad, score, token = call(
        functools.partial(grads_kernel, cap, 2 * LANES, (0, 2, 1, 3)),
        None,
        [(here, SMEM)] + [(x, VMEM) for x in (scaled, gate, up)] + [(w, HELD) for w in (own, beside, *others)],
        [(((total, ff), BF16), HELD)] * 2 + [(((groups, cap), F32), VMEM), (TOKEN, VMEM)],
        [
            pltpu.VMEM((ff, width), BF16),
            pltpu.VMEM((total, ff), BF16),
            pltpu.VMEM((total, ff), BF16),
            pltpu.VMEM((total, ff), F32),
            pltpu.VMEM((total, ff), F32),
            pltpu.VMEM((total, ff), BF16),
            pltpu.SemaphoreType.DMA((replicas,)),
            pltpu.SemaphoreType.DMA((2, -(-ff // (2 * LANES)))),
        ],
        (2 * total * width * ff, 2 * (total * width + ff * width + 4 * total * ff)),
        [far[-1]],
    )
    back = lax.all_to_all(
        score.reshape(groups, 1, cap), "expert", split_axis=0, concat_axis=0, tiled=True
    )
    (prob_grad,) = call(
        pick_kernel,
        1,
        [(back.reshape(groups, cap), fixed((groups, cap))), (dest, small), (prob, small)],
        [(((top, tok_rows), F32), small)],
        [],
        (total * tok_rows, total * LANES * 4),
        [token],
    )
    (near,) = call(
        near_kernel,
        1,
        [(scaled, fixed((total, width)))] + [(x, left) for x in near_mine] + [(x, half) for x in got],
        [(((part, width), F32), fixed((part, width)))],
        [],
        (2 * part * total * width, 8 * part * width),
        [token],
    )
    weight_grad = None
    for k in range(cuts):
        at = pl.BlockSpec((size, width), lambda i, k=k: (k, 0))
        (weight_grad,) = call(
            finish_kernel,
            1,
            [(near, at), (crossed[k], half)],
            [(((part, width), BF16), at)],
            [],
            (size * width, 8 * size * width),
            [] if k == 0 else [weight_grad],
            {} if k == 0 else {2: 0},
        )

    def bins(x):
        return jnp.transpose(x.reshape(cap, groups, ff), (1, 0, 2)).reshape(gate_saved.shape)

    return weight_grad[None], bins(gate_grad), bins(up_grad), prob_grad.T


def solution(mesh):
    placed = (
        P(("dp", "expert"), None),
        P(("dp", "expert"), None),
        P(("dp", "expert"), None),
        P(("dp", "expert"), None),
        P("dp", "expert", None, None, None),
        P("dp", "expert", None, None, None),
        P("expert", "dp", None),
    )
    return jax.shard_map(
        local,
        mesh=mesh,
        in_specs=placed,
        out_specs=(
            P("expert", "dp", None),
            P("dp", "expert", None, None, None),
            P("dp", "expert", None, None, None),
            P(("dp", "expert"), None),
        ),
        check_vma=False,
    )
```
